256 devices in a mesh: group: 16 (over z, x_hi), tp: 16 (over x_lo, y, core).
Axes of the slice: x: 4 (x_hi: 2, x_lo: 2; x = x_hi * 2 + x_lo), y: 4, z: 8, core: 2. Of those that a mesh axis runs over, the one named last changes fastest.
Arguments:
- hidden: bfloat16 [16, 16, 128, 8192], P('group', None, None, 'tp'), may hold values from -120 to 120
- norm_gain: bfloat16 [8192], P('tp'), may hold values from 0.099609375 to 1.8984375
- learner_weights: float32 [16, 8192, 2048], P('group', 'tp'), may hold values from -0.0625 to 0.0625
- plan: int32 [16, 16], P('group'), may hold values from 0 to 15, as said below
- block_fill: int32 [16, 16], P('group'), may hold values from 1 to 128
- block_pos: int32 [16, 16], P('group'), may hold values from 0 to 63
Outputs:
- kv_slots: bfloat16 [16, 32, 128, 2048], P('group', None, 'tp')
The draws below stay inside these ranges and needn't reach their ends.
Inputs may be any that keep to these rules, and one draw needn't show every extreme that they name: `plan`: no group sends more than 2 blocks to one group; in every draw one group receives exactly 2 blocks from every group.
All inputs are finite; a program needn't handle non-finite values.
Results may differ from the reference program's by a relative error of at most 0.023.
Values may be sent and summed in bfloat16 or wider, within the bound.
No kernel may reach another device: no remote copies, remote signals or barrier semaphores. Data moves between devices by JAX's collectives and lax.ppermute only.
A program may use at most 128 MiB of HBM per device.

```python
import math
import jax
import jax.numpy as jnp
from jax import lax

D = 8192
KV_HEADS = 8
HEAD = 128
BLOCK = 128
CAP = 2
BLK = 16
KVW = 2048
RECV = 32
N_GROUP = 16
N_TP = 16


def draw_hidden(key, part):
    key = jax.random.fold_in(key, 11)
    first_key, second_key, third_key = jax.random.split(key, 3)
    shape = (N_GROUP, BLK, BLOCK, D)
    base = jnp.clip(jax.random.normal(first_key, shape, jnp.float32), -4.0, 4.0)
    row_scale = jnp.exp(jax.random.uniform(second_key, (N_GROUP, BLK, BLOCK, 1), jnp.float32, 0.0, math.log(10.0)))
    rising = 3.0 ** (jnp.arange(D, dtype=jnp.float32) / D)
    column_scale = 0.5 * rising * jnp.exp(jax.random.uniform(third_key, (D,), jnp.float32, 0.0, math.log(2.0)))
    return (base * row_scale * column_scale).astype(jnp.bfloat16)


def draw_plan(key, part):
    key = jax.random.fold_in(key, 23)
    hot_key, offset_key, perm_key = jax.random.split(key, 3)
    hot_group = jax.random.randint(hot_key, (), 0, N_GROUP)
    offsets = jax.random.randint(offset_key, (N_GROUP, 1), 0, N_GROUP - 1)
    position = jnp.arange(BLK, dtype=jnp.int32)[None, :]
    others = (hot_group + 1 + (offsets + position - CAP) % (N_GROUP - 1)) % N_GROUP
    targets = jnp.where(position < CAP, hot_group, others)
    orders = jax.vmap(lambda single: jax.random.permutation(single, BLK))(jax.random.split(perm_key, N_GROUP))
    return jnp.take_along_axis(targets, orders, 1).astype(jnp.int32)


def plant(entries, own_key, low, largest):
    dims = entries.shape
    index_at = [jax.random.randint(jax.random.fold_in(own_key, axis), (), 0, dims[axis]) for axis in range(len(dims))]
    entries = entries.at[tuple(index_at)].set(low)
    longest = dims.index(max(dims))
    index_at[longest] = (index_at[longest] + 1) % dims[longest]
    return entries.at[tuple(index_at)].set(largest)


def shard_levels(stream_key, dims, cuts, smallest, largest):
    def one(dim, shards_of):
        draws = jax.random.uniform(jax.random.fold_in(jax.random.fold_in(stream_key, 6), dim), (shards_of,), jnp.float32, smallest / len(cuts), largest / len(cuts))
        return jnp.repeat(jnp.exp(draws), dims[dim] // shards_of).reshape((-1,) + (1,) * (len(dims) - dim - 1))

    loudness = one(*cuts[0])
    for cut in cuts[1:]:
        loudness = loudness * one(*cut)
    return loudness


def centred(own_key, extent, spread, bound, cuts=(), kind=jnp.bfloat16):
    drawn = jax.random.normal(own_key, extent, jnp.float32) * spread
    if len(cuts) > 0:
        drawn = shard_levels(own_key, extent, cuts, -0.22, 0.18) * drawn
    return jnp.clip(drawn, min=-bound, max=bound).astype(kind)


def setup_inputs(seed: int = 0) -> dict:
    streams_of = jax.random.split(jax.random.key(seed), 7)
    return {
        "hidden": draw_hidden(jax.random.fold_in(streams_of[6], 71), 0),
        "norm_gain": jnp.clip(1.0 + 0.18 * jax.random.normal(streams_of[1], (D,), jnp.float32), 0.099609375, 1.8984375).astype(jnp.bfloat16),
        "learner_weights": centred(streams_of[2], (N_GROUP, D, KVW), D ** -0.5, 0.0625, ((0, 16), (1, 16)), jnp.float32),
        "plan": draw_plan(jax.random.fold_in(streams_of[6], 71), 0),
        "block_fill": plant(jax.random.randint(streams_of[4], (N_GROUP, BLK), 1, BLOCK + 1), jax.random.fold_in(streams_of[4], 1), 1, BLOCK).astype(jnp.int32),
        "block_pos": plant(jax.random.randint(streams_of[5], (N_GROUP, BLK), 0, 64), jax.random.fold_in(streams_of[5], 1), 0, 63).astype(jnp.int32),
    }


def rotate(key_value, positions):
    half_width = HEAD // 2
    freqs = 500000.0 ** (-(jnp.arange(half_width, dtype=jnp.float32) * 2.0) / HEAD)
    angles = positions.astype(jnp.float32)[..., None, None] * freqs
    cosine = jnp.cos(angles)
    sine = jnp.sin(angles)
    keys_part = key_value[..., :KV_HEADS * HEAD].reshape(positions.shape + (KV_HEADS, HEAD))
    first = keys_part[..., :half_width]
    second = keys_part[..., half_width:]
    turned = jnp.concatenate([first * cosine - second * sine, second * cosine + first * sine], -1)
    turned = turned.reshape(positions.shape + (KV_HEADS * HEAD,))
    return jnp.concatenate([turned, key_value[..., KV_HEADS * HEAD:]], -1)

def reference(hidden, norm_gain, learner_weights, plan, block_fill, block_pos):
    weights = learner_weights[0].astype(jnp.bfloat16)
    values = hidden.astype(jnp.float32)
    mean_square = lax.optimization_barrier(jnp.sum(values * values, -1)) / D
    inverse = lax.rsqrt(mean_square + 1e-05)
    normed = (values * inverse[..., None] * norm_gain.astype(jnp.float32)).astype(jnp.bfloat16)
    rows_all = normed.reshape(-1, D)
    width_part = D // N_TP

    def add_part(summed, index):
        segment = lax.dynamic_slice_in_dim(rows_all, index * width_part, width_part, 1)
        weight_part = lax.dynamic_slice_in_dim(weights, index * width_part, width_part, 0)
        term = jnp.dot(segment, weight_part, preferred_element_type=jnp.float32).astype(jnp.bfloat16)
        term = lax.optimization_barrier(term)
        return (summed + term.astype(jnp.float32), None)
    summed, _ = lax.scan(add_part, jnp.zeros((rows_all.shape[0], KVW), jnp.float32), jnp.arange(N_TP, dtype=jnp.int32))
    key_value = summed.reshape(N_GROUP, BLK, BLOCK, KVW)
    token_index = jnp.arange(BLOCK, dtype=jnp.int32)
    positions = block_pos[..., None] * BLOCK + token_index
    rotated = rotate(key_value, positions)
    live_mask = token_index[None, None, :] < block_fill[..., None]
    finished = jnp.where(live_mask[..., None], rotated, 0.0).astype(jnp.bfloat16)
    one_hot = (plan[..., None] == jnp.arange(N_GROUP, dtype=jnp.int32)).astype(jnp.int32)
    earlier = jnp.cumsum(one_hot, 1) - one_hot
    slot_index = lax.optimization_barrier(jnp.sum(earlier * one_hot, -1)).astype(jnp.int32)
    sources = jnp.broadcast_to(jnp.arange(N_GROUP, dtype=jnp.int32)[:, None], plan.shape)
    target_slot = sources * CAP + slot_index
    output = jnp.zeros((N_GROUP, RECV, BLOCK, KVW), jnp.bfloat16)
    return output.at[plan, target_slot].set(finished)
```

```python
import functools

import jax
import jax.numpy as jnp
from jax import lax
from jax.experimental import pallas as pl
from jax.experimental.pallas import tpu as pltpu
from jax.sharding import PartitionSpec as P

D = 8192
KV_HEADS = 8
HEAD = 128
BLOCK = 128
CAP = 2
KVW = 2048
Z = 8
X = 2
Y = 4
PIECES = 8
PIECE = KVW // PIECES
CHUNKS = ((0, 1, 2, 3, 4), (5, 6, 7))
BF16 = jnp.bfloat16
F32 = jnp.float32


def tp_pairs(dx, dy, dc):
    pairs = []
    for t in range(16):
        x, y, c = t // 8, (t // 2) % 4, t % 2
        pairs.append((t, ((x ^ dx) * 4 + (y + dy) % Y) * 2 + (c ^ dc)))
    return pairs


def ring_pairs():
    pairs = []
    for g in range(16):
        for t in range(16):
            z, h, c = g // 2, g % 2, t % 2
            there = (z + (1 if c == 0 else -1)) % Z
            pairs.append((g * 16 + t, (there * 2 + h) * 16 + t))
    return pairs


def to_core(value):
    return lax.ppermute(value, "tp", tp_pairs(0, 0, 1))


def product_kernel(count, rows_ref, *refs):
    pieces, outs = refs[:count], refs[count:]
    for dy in range(Y):
        for k in range(count):
            outs[dy][:, k * PIECE : (k + 1) * PIECE] = jnp.dot(
                rows_ref[dy], pieces[k][...], preferred_element_type=F32
            ).astype(BF16)


def product(rows, pieces):
    count = len(pieces)
    half = rows.shape[1]
    width = count * PIECE
    vmem = pl.BlockSpec(memory_space=pltpu.VMEM)
    return pl.pallas_call(
        functools.partial(product_kernel, count),
        out_shape=[jax.ShapeDtypeStruct((half, width), BF16)] * Y,
        in_specs=[vmem] * (1 + count),
        out_specs=[vmem] * Y,
        compiler_params=pltpu.CompilerParams(vmem_limit_bytes=40 * 2**20),
        cost_estimate=pl.CostEstimate(
            flops=2 * Y * half * width * rows.shape[2],
            bytes_accessed=2 * (rows.size + width * rows.shape[2] + Y * half * width),
            transcendentals=0,
        ),
    )(rows, *pieces)


def finish_kernel(where_ref, source_ref, filled_ref, cos_ref, sin_ref, scale_ref, *refs):
    out_ref, done = refs[-2:]
    scale = scale_ref[...]
    at = 0
    for chunk in CHUNKS:
        parts, at = refs[at : at + Y + 1], at + Y + 1
        for n, k in enumerate(chunk):
            column = where_ref[k]
            is_key = jnp.where(column < PIECES // 2, 1.0, 0.0).astype(F32)
            for head in range(PIECE // HEAD):
                cols = slice(n * PIECE + head * HEAD, n * PIECE + (head + 1) * HEAD)
                value = parts[0][:, cols].astype(F32)
                for part in parts[1:]:
                    value = value + part[:, cols].astype(F32)
                other = pltpu.roll(value, HEAD // 2, 1)
                turned = value * cos_ref[...] + other * sin_ref[...]
                value = jnp.where(is_key > 0.5, turned, value) * scale
                start = pl.multiple_of(column * PIECE + head * HEAD, HEAD)
                done[:, pl.ds(start, HEAD)] = value
    tok = 8
    for group in range(out_ref.shape[0]):
        both = []
        for slot in range(CAP):
            j = group * CAP + slot
            first = pl.multiple_of(source_ref[j] * tok, tok)
            keep = filled_ref[j] > 0
            both.append(jnp.where(keep, done[pl.ds(first, tok), :], 0.0))
        out_ref[group] = jnp.concatenate(both, 0).astype(BF16)


def finish(column_of, source, filled, cosine, sine, scale, chunks, groups):
    rows = cosine.shape[0]
    smem = pl.BlockSpec(memory_space=pltpu.SMEM)
    vmem = pl.BlockSpec(memory_space=pltpu.VMEM)
    flat, specs = [], []
    for chunk in chunks:
        for part in chunk:
            flat.append(part)
            specs.append(pl.BlockSpec((rows, part.shape[1]), lambda i: (0, 0)))
    return pl.pallas_call(
        finish_kernel,
        grid=(1,),
        out_shape=jax.ShapeDtypeStruct((groups, CAP * 8, KVW), BF16),
        in_specs=[smem] * 3 + [vmem] * 3 + specs,
        out_specs=vmem,
        scratch_shapes=[pltpu.VMEM((rows, KVW), F32)],
        compiler_params=pltpu.CompilerParams(vmem_limit_bytes=40 * 2**20),
    )(column_of, source, filled, cosine, sine, scale, *flat)


def spread_weights(weights, group, core):
    z = group // 2
    pieces = [weights[:, k * PIECE : (k + 1) * PIECE] for k in range(PIECES)]
    own = jnp.where(group == 0, pieces[0], jnp.zeros_like(pieces[0]))
    for k in range(1, PIECES):
        own = own + lax.ppermute(pieces[k], "group", [(0, 2 * k)])
    own = own + lax.ppermute(own, "group", [(2 * k, 2 * k + 1) for k in range(Z)])
    partner = to_core(own)
    first = core == 0
    own = jnp.concatenate([jnp.where(first, own, partner), jnp.where(first, partner, own)], 0)
    held = [own]
    moving = own
    for step in range(1, Z // 2):
        moving = lax.ppermute(moving, ("group", "tp"), ring_pairs())
        held += [moving, to_core(moving)]
    features = weights.shape[0]
    half = lax.dynamic_slice_in_dim(moving, core * features, features, 0)
    half = lax.ppermute(half, ("group", "tp"), ring_pairs())
    partner = to_core(half)
    held.append(
        jnp.concatenate([jnp.where(first, half, partner), jnp.where(first, partner, half)], 0)
    )
    sign = jnp.where(first, -1, 1)
    steps = [0]
    for step in range(1, Z // 2):
        steps += [step, -step]
    steps.append(Z // 2)
    column_of = (z + sign * jnp.array(steps, jnp.int32) + Z) % Z
    return held, column_of.astype(jnp.int32)


def body(hidden, norm_gain, learner_weights, plan, block_fill, block_pos):
    groups = lax.axis_size("group")
    slots_total = groups * CAP
    blocks = hidden.shape[1]
    features = hidden.shape[3]
    group = lax.axis_index("group")
    tp = lax.axis_index("tp")
    x, y, core = tp // 8, (tp // 2) % Y, tp % 2
    tok = BLOCK // 16
    rows = blocks * tok

    weights = learner_weights[0].astype(BF16).astype(F32) * norm_gain.astype(F32)[:, None]
    held, column_of = spread_weights(weights.astype(BF16), group, core)

    by_owner = hidden[0].reshape(blocks, 16, tok, features).transpose(1, 0, 2, 3)
    dy = jnp.arange(Y, dtype=jnp.int32)[:, None]
    dx = jnp.arange(X, dtype=jnp.int32)[None, :]
    owner = ((x ^ dx) * Y + (y + dy) % Y).reshape(-1) * 2
    mine = jnp.take(by_owner, owner + core, axis=0)
    theirs = to_core(jnp.take(by_owner, owner + 1 - core, axis=0))
    first = core == 0
    rows_all = jnp.concatenate(
        [jnp.where(first, mine, theirs), jnp.where(first, theirs, mine)], -1
    ).reshape(Y, X * rows, 2 * features)

    squares = jnp.sum(jnp.square(rows_all.astype(F32)), -1).reshape(Y, X, rows)
    total = squares[0]
    for step in range(1, Y):
        total = total + lax.ppermute(squares[step], "tp", tp_pairs(0, step, 0))
    total = total[0] + lax.ppermute(total[1], "tp", tp_pairs(1, 0, 0))
    inverse = lax.rsqrt(total / D + 1e-05)

    token = tp * tok + jnp.arange(tok, dtype=jnp.int32)
    positions = (block_pos[0][:, None] * BLOCK + token[None, :]).reshape(rows)
    live = (token[None, :] < block_fill[0][:, None]).reshape(rows)
    half_width = HEAD // 2
    freqs = 500000.0 ** (-(jnp.arange(half_width, dtype=F32) * 2.0) / HEAD)
    angles = positions.astype(F32)[:, None] * freqs
    cosine, sine = jnp.cos(angles), jnp.sin(angles)
    cosine = jnp.concatenate([cosine, cosine], -1)
    sine = jnp.concatenate([-sine, sine], -1)
    scale = jnp.where(live, inverse, 0.0)[:, None]

    targets = plan[0]
    one_hot = (targets[:, None] == jnp.arange(groups, dtype=jnp.int32)[None, :]).astype(jnp.int32)
    earlier = jnp.cumsum(one_hot, 0) - one_hot
    target_slot = targets * CAP + jnp.sum(earlier * one_hot, -1)
    matches = target_slot[None, :] == jnp.arange(slots_total, dtype=jnp.int32)[:, None]
    filled = jnp.any(matches, 1).astype(jnp.int32)
    source = jnp.sum(
        matches.astype(jnp.int32) * jnp.arange(blocks, dtype=jnp.int32)[None, :], 1
    )

    chunks = []
    for chunk in CHUNKS:
        parts = product(rows_all, [held[k] for k in chunk])
        summed = [parts[0]]
        for step in range(1, Y):
            summed.append(lax.ppermute(parts[step], "tp", tp_pairs(0, step, 0)))
        away = sum(part[rows:].astype(F32) for part in summed).astype(BF16)
        summed.append(lax.ppermute(away, "tp", tp_pairs(1, 0, 0)))
        chunks.append(summed)

    outgoing = finish(column_of, source, filled, cosine, sine, scale, chunks, groups)
    result = lax.all_to_all(outgoing, "group", split_axis=0, concat_axis=0, tiled=True)
    return result.reshape(1, slots_total, tok, KVW)


def solution(mesh):
    in_specs = (
        P("group", None, None, "tp"),
        P("tp"),
        P("group", "tp", None),
        P("group", None),
        P("group", None),
        P("group", None),
    )
    out_specs = P("group", None, "tp", None)
    return jax.shard_map(body, mesh=mesh, in_specs=in_specs, out_specs=out_specs, check_vma=False)
```

```python
import functools

import jax
import jax.numpy as jnp
from jax import lax
from jax.experimental import pallas as pl
from jax.experimental.pallas import tpu as pltpu
from jax.sharding import PartitionSpec as P

D = 8192
HEAD = 128
BLOCK = 128
CAP = 2
KVW = 2048
Z = 8
X = 2
Y = 4
PIECES = 8
EARLY = 10
EXTRA = 16
BF16 = jnp.bfloat16
F32 = jnp.float32
I32 = jnp.int32
VMEM = pl.BlockSpec(memory_space=pltpu.VMEM)
SMEM = pl.BlockSpec(memory_space=pltpu.SMEM)
ANY = pl.BlockSpec(memory_space=pl.ANY)
HBM = pl.BlockSpec(memory_space=pltpu.HBM)


def tp_pairs(dx, dy, dc):
    pairs = []
    for t in range(16):
        x, y, c = t // 8, (t // 2) % 4, t % 2
        pairs.append((t, ((x ^ dx) * 4 + (y + dy) % Y) * 2 + (c ^ dc)))
    return pairs


def ring_pairs(cores):
    pairs = []
    for g in range(16):
        for t in range(16):
            z, h, c = g // 2, g % 2, t % 2
            there = (z + (1 if c == 0 else -1)) % Z
            if c in cores:
                pairs.append((g * 16 + t, (there * 2 + h) * 16 + t))
    return pairs


def to_core(value):
    return lax.ppermute(value, "tp", tp_pairs(0, 0, 1))


def load(sources, targets, sem, first=0):
    copies = [
        pltpu.make_async_copy(source, target, sem.at[first + n])
        for n, (source, target) in enumerate(zip(sources, targets, strict=True))
    ]
    for copy in copies:
        copy.start()
    return copies


def wait(copies):
    for copy in copies:
        copy.wait()


def buffers(shapes, count):
    return [pltpu.VMEM(shape, dtype) for shape, dtype in shapes] + [pltpu.SemaphoreType.DMA((count,))]


def like(arrays):
    return [(array.shape, array.dtype) for array in arrays]


def params(mib):
    return pltpu.CompilerParams(vmem_limit_bytes=mib * 2**20)


def weights_kernel(gain_ref, weights_ref, *outs):
    rows = weights_ref.shape[0]
    gain = gain_ref[...].astype(F32)
    down = lax.broadcasted_iota(I32, (rows, rows), 0)
    across = lax.broadcasted_iota(I32, (rows, rows), 1)
    gain = jnp.sum(jnp.where(down == across, gain, 0.0), 1, keepdims=True)
    for k, out in enumerate(outs):
        for half in range(2):
            first = half * (KVW // 2) + k * HEAD
            part = weights_ref[:, first : first + HEAD].astype(BF16).astype(F32)
            out[half] = (part * gain).astype(BF16)


def weight_pieces(gain, weights):
    features, step = weights.shape[0], 256
    return pl.pallas_call(
        weights_kernel,
        grid=(features // step,),
        out_shape=[jax.ShapeDtypeStruct((2, features, HEAD), BF16)] * PIECES,
        in_specs=[
            pl.BlockSpec((1, step), lambda i: (0, i)),
            pl.BlockSpec((step, KVW), lambda i: (i, 0)),
        ],
        out_specs=[pl.BlockSpec((2, step, HEAD), lambda i: (0, i, 0))] * PIECES,
        compiler_params=pltpu.CompilerParams(vmem_limit_bytes=60 * 2**20),
    )(gain[None, :], weights)


def combine_kernel(learner_ref, *refs):
    pieces, out, (held, sem) = refs[:PIECES], refs[-3], refs[-2:]
    copies = load(pieces, [held.at[k] for k in range(PIECES)], sem)
    wait(copies)
    total = jnp.where(learner_ref[0] > 0, held[0], jnp.zeros_like(held[0]))
    for k in range(1, PIECES):
        total = total + held[k]
    held[0] = total
    wait(load([held.at[0]], [out], sem))


def combine(learner, pieces, others):
    shape = pieces[0].shape
    return pl.pallas_call(
        combine_kernel,
        out_shape=jax.ShapeDtypeStruct(shape, BF16),
        in_specs=[SMEM] + [HBM] * PIECES + [ANY] * len(others),
        out_specs=HBM,
        scratch_shapes=buffers([((PIECES,) + shape, BF16)], PIECES),
        compiler_params=params(60),
    )(learner, *pieces, *others)


def spread_weights(pieces, group, x, others):
    z = group // 2
    arrived = [lax.ppermute(pieces[k], "group", [(0, 2 * k)]) for k in (4, 5, 3, 6, 2, 7, 1)]
    learner = (group == 0).astype(I32)[None]
    own = combine(learner, [pieces[0]] + arrived, others)
    own = own + lax.ppermute(own, "group", [(2 * k, 2 * k + 1) for k in range(Z)])
    first = x == 0
    same, other = jnp.where(first, own[0], own[1]), jnp.where(first, own[1], own[0])
    arrived = over_x(other)
    diagonal = lax.ppermute(other, "tp", tp_pairs(1, 0, 1))
    held = [jnp.concatenate([same, to_core(same), arrived, diagonal], 0)]
    for step in range(1, 4):
        held.append(lax.ppermute(held[-1], ("group", "tp"), ring_pairs((0, 1))))
    return held, arrived


def product_kernel(count, extra, where_ref, *refs):
    tokens, pieces = refs[:6], refs[6 : 6 + count]
    results, (rows, thin, wide, held, sem) = refs[-5 - Y : -5], refs[-5:]
    features = rows.shape[-1]
    weights = load(pieces, [thin.at[k] for k in range(count)], sem)
    copies = []
    for dy in range(Y):
        owner = lax.rem(where_ref[0] + dy, Y)
        sources = [token.at[:, :, owner] for token in tokens]
        targets = [rows.at[dy, 0], rows.at[dy, 1]]
        for n in (2, 3):
            targets += [rows.at[dy, n, :EARLY], rows.at[dy, n, EARLY:]]
        copies.append(load(sources, targets, sem, count + 6 * dy))
    wait(weights)
    first = where_ref[1] == 0
    for k in range(count - 1):
        wide[:, k * HEAD : (k + 1) * HEAD] = jnp.where(first, thin[k], thin[k + 1])
    out = []
    for dy in range(Y):
        wait(copies[dy])
        total = None
        for n in range(4):
            term = jnp.dot(
                rows[dy, n].reshape(-1, features),
                wide[n * features : (n + 1) * features, :],
                preferred_element_type=F32,
            )
            total = term if total is None else total + term
        held[dy, : total.shape[0], :] = total.astype(BF16)
        if extra:
            held[dy, total.shape[0] :, :] = refs[6 + count][dy]
        out += load([held.at[dy]], [results[dy]], sem, dy)
    wait(out)


def product(where, tokens, pieces, lines=(), others=()):
    count = len(pieces)
    blocks, tok, features = tokens[0].shape[0], tokens[0].shape[3], tokens[0].shape[4]
    rows = blocks * X * tok
    sent = rows + EXTRA * len(lines)
    depth, width = pieces[0].shape[0], (count - 1) * HEAD
    return pl.pallas_call(
        functools.partial(product_kernel, count, len(lines)),
        out_shape=[jax.ShapeDtypeStruct((sent, width), BF16)] * Y,
        in_specs=[SMEM] + [HBM] * (6 + count) + [VMEM] * len(lines) + [ANY] * len(others),
        out_specs=[HBM] * Y,
        scratch_shapes=buffers(
            [
                ((Y, 4, blocks, X, tok, features), BF16),
                ((count, depth, HEAD), BF16),
                ((depth, width), BF16),
                ((Y, sent, width), BF16),
            ],
            count + 6 * Y,
        ),
        compiler_params=params(60),
        cost_estimate=pl.CostEstimate(
            flops=2 * Y * rows * width * depth,
            bytes_accessed=2 * (Y * rows * depth + width * depth + Y * rows * width),
            transcendentals=0,
        ),
    )(where, *tokens, *pieces, *lines, *others)


def add_kernel(*refs):
    parts, out, (held, total, sem) = refs[:Y], refs[Y], refs[-3:]
    wait(load(parts, [held.at[n] for n in range(Y)], sem))
    total[...] = sum(held[n].astype(F32) for n in range(Y))
    wait(load([total], [out], sem))


def add(parts):
    shape = parts[0].shape
    return pl.pallas_call(
        add_kernel,
        out_shape=jax.ShapeDtypeStruct(shape, F32),
        in_specs=[HBM] * Y,
        out_specs=HBM,
        scratch_shapes=buffers([((Y,) + shape, BF16), (shape, F32)], Y),
        compiler_params=params(60),
    )(*parts)


def share_kernel(where_ref, summed_ref, *refs):
    parts, results, (summed, held, both, sent, line, sem) = refs[:Y], refs[Y : Y + 5], refs[-6:]
    copies = load(parts, [held.at[n] for n in range(Y)], sem)
    copies += load([summed_ref], [summed], sem, Y)
    wait(copies)
    width = summed.shape[-1]
    rows = summed.shape[0] - EXTRA
    both[..., :width] = summed[:rows].reshape(both.shape[:-1] + (width,))
    late = sum(held[n].astype(F32) for n in range(Y))
    both[..., width:] = late.reshape(both.shape[:-1] + (width,))
    total = summed[rows : rows + 2] + summed[rows + 2 : rows + 4]
    line[...] = total
    high = total.astype(BF16).astype(F32)
    extra = jnp.concatenate([high, total - high], 1)
    extra = jnp.concatenate([extra, jnp.zeros((EXTRA - 2, 2 * width), F32)], 0)
    x, core = where_ref[2], where_ref[1]
    copies = load([line], [results[4]], sem, 4)
    for n in (3, 2, 1, 0):
        chip = x if n < 2 else 1 - x
        of_core = core if n % 2 == 0 else 1 - core
        value = both[:, chip, of_core].reshape(-1, 2 * width)
        size = value.shape[0]
        sent[n, :size] = value.astype(BF16)
        if n == 2:
            sent[n, size:] = extra.astype(BF16)
            size += EXTRA
        copies += load([sent.at[n, :size]], [results[n]], sem, n)
    wait(copies)


def share(where, summed, parts, blocks, tok):
    width = 2 * summed.shape[1]
    rows = [blocks * tok + (EXTRA if n == 2 else 0) for n in range(4)]
    return pl.pallas_call(
        share_kernel,
        out_shape=[jax.ShapeDtypeStruct((each, width), BF16) for each in rows]
        + [jax.ShapeDtypeStruct((2, width // 2), F32)],
        in_specs=[SMEM] + [HBM] * (1 + Y),
        out_specs=[HBM] * 5,
        scratch_shapes=buffers(
            [
                (summed.shape, F32),
                ((Y,) + parts[0].shape, BF16),
                ((blocks, X, 2, tok, width), F32),
                ((4, rows[2], width), BF16),
                ((2, width // 2), F32),
            ],
            Y + 1,
        ),
        compiler_params=params(60),
    )(where, summed, *parts)


def after(values, others):
    count = len(values)
    return pl.pallas_call(
        lambda *refs: None,
        out_shape=[jax.ShapeDtypeStruct(value.shape, value.dtype) for value in values],
        in_specs=[ANY] * (count + len(others)),
        out_specs=[ANY] * count,
        input_output_aliases={i: i for i in range(count)},
    )(*values, *others)


def over_y(parts):
    return [parts[0]] + [
        lax.ppermute(parts[step], "tp", tp_pairs(0, step, 0)) for step in range(1, Y)
    ]


def over_x(value):
    return lax.ppermute(value, "tp", tp_pairs(1, 0, 0))


def squares_kernel(where_ref, mine_ref, theirs_ref, out, mine, theirs, sem):
    features = mine.shape[-1]
    wait(load([mine_ref, theirs_ref], [mine, theirs], sem))
    step = 128
    down = lax.broadcasted_iota(I32, (step, step), 0)
    across = lax.broadcasted_iota(I32, (step, step), 1)
    for dy in range(Y):
        owner = lax.rem(where_ref[0] + dy, Y)
        total = 0.0
        for token in (mine, theirs):
            rows = token[:, :, owner].reshape(-1, features).astype(F32)
            total = total + jnp.sum(rows * rows, 1, keepdims=True)
        lines = []
        for at in range(0, total.shape[0], step):
            turned = jnp.where(down == across, total[at : at + step], 0.0)
            lines.append(jnp.sum(turned, 0, keepdims=True))
        half = len(lines) // 2
        lines = [jnp.concatenate(lines[:half], 1), jnp.concatenate(lines[half:], 1)]
        lines = jnp.concatenate(lines, 0)
        high = lines.astype(BF16).astype(F32)
        rest = jnp.zeros((EXTRA - 4, lines.shape[1]), F32)
        out[dy] = jnp.concatenate([high, lines - high, rest], 0).astype(BF16)


def sums_of_squares(where, mine, theirs):
    rows = mine.shape[0] * X * mine.shape[3]
    return pl.pallas_call(
        squares_kernel,
        out_shape=jax.ShapeDtypeStruct((Y, EXTRA, rows // 2), BF16),
        in_specs=[SMEM] + [HBM] * 2,
        out_specs=VMEM,
        scratch_shapes=buffers(like([mine, theirs]), 2),
        compiler_params=params(60),
    )(where, mine, theirs)


def cut_kernel(begin, end, tokens_ref, *refs):
    out, held, sem = refs[-3:]
    wait(load([tokens_ref.at[begin:end]], [held], sem))
    wait(load([held], [out], sem))


def cut(tokens, begin, end, others=()):
    shape = (end - begin,) + tokens.shape[1:]
    return pl.pallas_call(
        functools.partial(cut_kernel, begin, end),
        out_shape=jax.ShapeDtypeStruct(shape, BF16),
        in_specs=[HBM] + [ANY] * len(others),
        out_specs=HBM,
        scratch_shapes=buffers([(shape, BF16)], 1),
        compiler_params=params(60),
    )(tokens, *others)


def finish_kernel(where_ref, source_ref, filled_ref, lines_ref, live_ref, cos_ref, sin_ref, *refs):
    sources, result, out_ref, done, parts, sem = refs[:4], refs[4], refs[5], refs[6], refs[7:11], refs[11]
    wait(load(sources, parts, sem))
    rows = cos_ref.shape[1]
    width = lines_ref.shape[1]
    arrived = parts[2][rows : rows + 2].astype(F32)
    total = lines_ref[...] + arrived[:, :width] + arrived[:, width:]
    inverse = lax.rsqrt(total / D + 1e-05)
    row = lax.broadcasted_iota(I32, (rows, width), 0)
    at = lax.broadcasted_iota(I32, (rows, width), 1)
    half = rows // 2
    tok = 8
    wanted = (row % half // tok) * 4 * tok + (where_ref[2] * 2 + where_ref[1]) * tok + row % tok
    lines = jnp.where(row < half, inverse[:1], inverse[1:])
    scale = jnp.sum(jnp.where(at == wanted, lines, 0.0), 1, keepdims=True)
    scale = jnp.where(live_ref[...] > 0, scale, 0.0)
    z, core, x = where_ref[3], where_ref[1], where_ref[2]
    for n, part in enumerate(parts):
        kind = x if n < 2 else 1 - x
        of_core = core if n % 2 == 0 else 1 - core
        for k in range(part.shape[1] // HEAD):
            value = part[:rows, k * HEAD : (k + 1) * HEAD].astype(F32) * scale
            other = pltpu.roll(value, HEAD // 2, 1)
            head = lax.rem(jnp.where(of_core == 0, z + PIECES - k, z + 1 + k), PIECES)
            start = pl.multiple_of((kind * PIECES + head) * HEAD, HEAD)
            done[:, pl.ds(start, HEAD)] = value * cos_ref[kind] + other * sin_ref[kind]
    copies = []
    for group in range(out_ref.shape[0]):
        both = []
        for j in range(group * CAP, (group + 1) * CAP):
            first = pl.multiple_of(source_ref[j] * tok, tok)
            both.append(jnp.where(filled_ref[j] > 0, done[pl.ds(first, tok), :], 0.0))
        out_ref[group] = jnp.concatenate(both, 0).astype(BF16)
        if group % 4 == 3:
            some = pl.ds(group - 3, 4)
            copies += load([out_ref.at[some]], [result.at[some]], sem, group // 4)
    wait(copies)


def finish(where, source, filled, lines, live, cosine, sine, parts, groups):
    shape = (groups, CAP * 8, KVW)
    return pl.pallas_call(
        finish_kernel,
        out_shape=jax.ShapeDtypeStruct(shape, BF16),
        in_specs=[SMEM] * 3 + [VMEM] * 4 + [HBM] * len(parts),
        out_specs=HBM,
        scratch_shapes=buffers(
            [(shape, BF16), ((cosine.shape[1], KVW), F32), *like(parts)], len(parts)
        ),
        compiler_params=params(60),
    )(where, source, filled, lines, live, cosine, sine, *parts)


def slots_of(plan, groups):
    blocks = plan.shape[0]
    one_hot = (plan[:, None] == jnp.arange(groups, dtype=I32)[None, :]).astype(I32)
    earlier = jnp.cumsum(one_hot, 0) - one_hot
    target_slot = plan * CAP + jnp.sum(earlier * one_hot, -1)
    matches = target_slot[None, :] == jnp.arange(groups * CAP, dtype=I32)[:, None]
    filled = jnp.any(matches, 1).astype(I32)
    source = jnp.sum(matches.astype(I32) * jnp.arange(blocks, dtype=I32)[None, :], 1)
    return source, filled


def body(hidden, norm_gain, learner_weights, plan, block_fill, block_pos):
    groups = lax.axis_size("group")
    blocks = hidden.shape[1]
    features = hidden.shape[3]
    group = lax.axis_index("group")
    tp = lax.axis_index("tp")
    x, y, core = tp // 8, (tp // 2) % Y, tp % 2
    tok = BLOCK // 16
    rows = blocks * tok

    pieces = weight_pieces(norm_gain, learner_weights[0])

    where = jnp.stack([y, core, x, group // 2]).astype(I32)
    mine = hidden[0].reshape(blocks, X, Y, 2 * tok, features)
    theirs = to_core(mine)
    early = over_x(cut(mine, 0, EARLY))
    late = cut(mine, EARLY, blocks, [pieces[0]])
    squares = sums_of_squares(where, mine, theirs)
    held, arrived = spread_weights(pieces, group, x, [early, late, squares])
    (late,) = after([late], [arrived])
    late = over_x(late)
    tokens = [mine, theirs, early, late, to_core(early), to_core(late)]

    first_parts = product(where, tokens, held[:3], [squares])
    (held[3],) = after([held[3]], [first_parts[1]])
    held.append(lax.ppermute(held[3], ("group", "tp"), ring_pairs((1,))))
    first_parts = over_y(first_parts)
    second_parts = over_y(product(where, tokens, held[2:], [], [first_parts[1]]))
    kept, *away, lines = share(where, add(first_parts), second_parts, blocks, tok)
    parts = [kept, to_core(away[0]), over_x(away[1])]
    parts.append(lax.ppermute(away[2], "tp", tp_pairs(1, 0, 1)))

    token = tp * tok + jnp.arange(tok, dtype=I32)
    positions = (block_pos[0][:, None] * BLOCK + token).reshape(rows)
    live = (token < block_fill[0][:, None]).reshape(rows, 1).astype(F32)
    half_width = HEAD // 2
    freqs = 500000.0 ** (-(jnp.arange(half_width, dtype=F32) * 2.0) / HEAD)
    angles = positions.astype(F32)[:, None] * freqs
    cosine, sine = jnp.cos(angles), jnp.sin(angles)
    cosine = jnp.concatenate([cosine, cosine], -1)
    sine = jnp.concatenate([-sine, sine], -1)
    cosine = jnp.stack([cosine, jnp.ones_like(cosine)])
    sine = jnp.stack([sine, jnp.zeros_like(sine)])
    source, filled = slots_of(plan[0], groups)

    outgoing = finish(where, source, filled, lines, live, cosine, sine, parts, groups)
    got = lax.all_to_all(outgoing, "group", split_axis=0, concat_axis=0, tiled=True)
    return got.reshape(1, groups * CAP, tok, KVW)


def solution(mesh):
    in_specs = (
        P("group", None, None, "tp"),
        P("tp"),
        P("group", "tp", None),
        P("group", None),
        P("group", None),
        P("group", None),
    )
    out_specs = P("group", None, "tp", None)
    return jax.shard_map(body, mesh=mesh, in_specs=in_specs, out_specs=out_specs, check_vma=False)
```
